32 devices in a mesh: grp: 2 (over y), pix: 4 (over z), ori: 2 (over x), pat: 2 (over core).
Axes of the slice: x: 2, y: 2, z: 4, core: 2. Of those that a mesh axis runs over, the one named last changes fastest.
Arguments:
- patterns: bfloat16 [2048, 65536], P(('grp', 'pat'), 'pix'), parts along dimension 0, may hold values from -40 to 40
- model: bfloat16 [131072, 2048], P(('grp', 'pix'), 'ori'), parts along dimension 0, may hold values from -6 to 6
- scale_table: float32 [32], P('grp'), parts along dimension 0, may hold values from 0.5 to 2
- scale_index: int32 [2048], P(('grp', 'pat')), parts along dimension 0, may hold values from 0 to 15
- weight_table: float32 [16], P('grp'), parts along dimension 0, may hold values from -1 to 1
- weight_class: int32 [4096], P(('grp', 'ori')), parts along dimension 0, may hold values from 0 to 7
Outputs:
- new_model: bfloat16 [131072, 2048], P(('grp', 'pix', 'pat'), 'ori'), parts along dimension 0
The draws below stay inside these ranges and needn't reach their ends.
There are 2 independent parts, one for each index of `grp`. The reference program is written for one: setup_inputs(seed, part) draws one part's arguments, and reference() takes and returns one part's arrays. A program takes and returns all parts, laid end to end along the dimension named above; each array names one. Nothing has to cross between parts.
All inputs are finite; a program needn't handle non-finite values.
Results may differ from the reference program's by a relative error of at most 0.0034.
Values may be sent and summed in bfloat16 or wider, within the bound.
A program may use at most 256 MiB of HBM per device.

```python
import math
import jax
import jax.numpy as jnp
from jax import lax

P_SIZE = 65536
R = 2048
S = 16
Q = 8
N = 1024


def slice_base(key):
    return jnp.clip(jax.random.normal(jax.random.fold_in(key, 17), (P_SIZE, R), jnp.float32), -6.0, 6.0)


def draw_model(key, part):
    return slice_base(key).astype(jnp.bfloat16)


def draw_patterns(key, part):
    noise = jax.random.normal(jax.random.fold_in(key, 23), (N, P_SIZE), jnp.float32)
    base = slice_base(key)
    first = jax.random.randint(jax.random.fold_in(key, 31), (N,), 0, R)
    second = jax.random.randint(jax.random.fold_in(key, 37), (N,), 0, R)
    strength = jnp.array([1.5, 2.0, 3.0], jnp.float32)[jnp.arange(N) % 3]
    aligned = strength[:, None] * (base[:, first].T + base[:, second].T) + noise
    special = jnp.arange(N) % 16 == 0
    values = jnp.where(special[:, None], aligned, noise)
    return jnp.clip(values, -40.0, 40.0).astype(jnp.bfloat16)


def set_ends(entries, own_key, low, top_value):
    shape = entries.shape
    place = [jax.random.randint(jax.random.fold_in(own_key, axis), (), 0, shape[axis]) for axis in range(len(shape))]
    entries = entries.at[tuple(place)].set(low)
    longest = shape.index(max(shape))
    place[longest] = (place[longest] + 1) % shape[longest]
    return entries.at[tuple(place)].set(top_value)


def setup_inputs(seed: int = 0, part: int = 0) -> dict:
    key_of = jax.random.split(jax.random.key(seed), 7)
    own_keys = jax.random.split(jax.random.fold_in(key_of[6], part), 7)
    return {
        "patterns": draw_patterns(jax.random.fold_in(jax.random.fold_in(key_of[6], part), 71), part),
        "model": draw_model(jax.random.fold_in(jax.random.fold_in(key_of[6], part), 71), part),
        "scale_table": jnp.clip(jnp.exp(jax.random.uniform(own_keys[2], (S,), jnp.float32, math.log(0.5), math.log(2.0))), 0.5, 2.0),
        "scale_index": set_ends(jax.random.randint(own_keys[3], (N,), 0, S), jax.random.fold_in(own_keys[3], 1), 0, S - 1).astype(jnp.int32),
        "weight_table": jnp.clip(jax.random.uniform(own_keys[4], (Q,), jnp.float32, -1.0, 1.0), -1.0, 1.0),
        "weight_class": set_ends(jax.random.randint(own_keys[5], (R,), 0, Q), jax.random.fold_in(own_keys[5], 1), 0, Q - 1).astype(jnp.int32),
    }


prior_weight = 0.5


def reference(patterns, model, scale_table, scale_index, weight_table, weight_class):
    levels = jnp.arange(scale_table.shape[0], dtype=jnp.int32)
    phi = jnp.sum(jnp.where(scale_index[:, None] == levels[None, :], scale_table[None, :], 0.0), axis=1)
    classes = jnp.arange(weight_table.shape[0], dtype=jnp.int32)
    logw = jnp.sum(jnp.where(weight_class[:, None] == classes[None, :], weight_table[None, :], 0.0), axis=1)
    cross = jnp.dot(patterns, model, preferred_element_type=jnp.float32)
    squares = jnp.sum(jnp.square(model.astype(jnp.float32)), axis=0)
    beta = P_SIZE ** -0.5
    scores = beta * (phi[:, None] * cross - 0.5 * (phi * phi)[:, None] * squares[None, :]) + logw[None, :]
    top = jnp.max(scores, axis=1)
    lse = top + jnp.log(jnp.sum(jnp.exp(scores - top[:, None]), axis=1))
    prob = jnp.exp(scores - lse[:, None])
    weights = (prob * phi[:, None]).astype(jnp.bfloat16)
    den = prior_weight + jnp.sum(prob * (phi * phi)[:, None], axis=0)
    numer = lax.dot_general(patterns, weights, (((0,), (0,)), ((), ())), preferred_element_type=jnp.float32)
    numer = numer + prior_weight * model.astype(jnp.float32)
    return (numer / den[None, :]).astype(jnp.bfloat16)
```

```python
import functools

import jax
import jax.numpy as jnp
from jax import lax
from jax.experimental import pallas as pl
from jax.experimental.pallas import tpu as pltpu
from jax.sharding import PartitionSpec as P

prior_weight = 0.5
MESH = pl.DeviceIdType.MESH
F32 = jnp.float32
BF16 = jnp.bfloat16


def table_lookup(table, index):
    levels = jnp.arange(table.shape[0], dtype=jnp.int32)
    return jnp.sum(jnp.where(index[:, None] == levels[None, :], table[None, :], 0.0), axis=1)


def block_of(size, most):
    block = min(size, most)
    while size % block:
        block //= 2
    return block


def score_kernel(
    n_pix, n_ori, beta, chunks, width, steps, depth, slots,
    pat_hbm, model_hbm, phi_ref, logw_ref,
    w_ref, den_ref, sib_ref,
    pat_v, mbuf, acc, sq, part, rx, sc, st, dpart,
    pat_sem, m_sem, sib_sem, rs_send, rs_recv, st_send, st_recv,
    agz_send, agz_recv, ags_send, ags_recv,
):
    z = lax.axis_index("pix")
    core = lax.axis_index("pat")
    ori = lax.axis_index("ori")
    last = n_pix - 1
    half_rows = part.shape[2]
    sub = half_rows // 2
    units = chunks * 2
    hops = (z, last - z)
    nexts = (lax.rem(z + 1, n_pix), lax.rem(z + n_pix - 1, n_pix))

    def model_copy(j):
        c, k = j // steps, j % steps
        return pltpu.make_async_copy(
            model_hbm.at[pl.ds(k * depth, depth), pl.ds(c * width, width)],
            mbuf.at[j % slots], m_sem.at[j % slots])

    def pattern_copy(k):
        cols = pl.ds(k * depth, depth)
        return pltpu.make_async_copy(pat_hbm.at[:, cols], pat_v.at[:, cols], pat_sem.at[k])

    total_steps = chunks * steps
    for k in range(steps):
        pattern_copy(k).start()
        if k < min(slots, total_steps):
            model_copy(k).start()
    for j in range(steps, min(slots, total_steps)):
        model_copy(j).start()

    barrier = pltpu.get_barrier_semaphore()
    for d in range(2):
        @pl.when(hops[d] < last)
        def _():
            pl.semaphore_signal(barrier, inc=1, device_id={"pix": nexts[d]}, device_id_type=MESH)
    pl.semaphore_signal(barrier, inc=1, device_id={"pat": 1 - core}, device_id_type=MESH)
    for k in range(1, n_ori):
        pl.semaphore_signal(
            barrier, inc=1, device_id={"ori": lax.rem(ori + k, n_ori)}, device_id_type=MESH)
    @pl.when(hops[0] * hops[1] == 0)
    def _():
        pl.semaphore_wait(barrier, n_ori + 1)

    @pl.when(hops[0] * hops[1] > 0)
    def _():
        pl.semaphore_wait(barrier, n_ori + 2)

    half_pix = sib_ref.shape[1]
    sib_copy = pltpu.make_async_remote_copy(
        src_ref=pat_hbm.at[:, pl.ds((1 - core) * half_pix, half_pix)], dst_ref=sib_ref,
        send_sem=sib_sem.at[0], recv_sem=sib_sem.at[1],
        device_id={"pat": 1 - core}, device_id_type=MESH)

    def rows_of(s):
        return pl.ds(s * sub, sub)

    def rs_copy(d, u):
        c, s = divmod(u, 2)
        return pltpu.make_async_remote_copy(
            src_ref=part.at[d, c, rows_of(s)], dst_ref=rx.at[d, c, rows_of(s)],
            send_sem=rs_send.at[d, u], recv_sem=rs_recv.at[d, u],
            device_id={"pix": nexts[d]}, device_id_type=MESH)

    def relay(d, u):
        c, s = divmod(u, 2)
        rs_copy(d, u).wait_recv()
        rows = rows_of(s)

        @pl.when(hops[d] < last)
        def _():
            part[d, c, rows] = part[d, c, rows] + rx[d, c, rows]
            rs_copy(d, u).start()

        @pl.when(hops[d] == last)
        def _():
            cols = pl.ds(c * width, width)
            sc[rows, cols] = part[d, c, rows] + rx[d, c, rows] + logw_ref[:, cols]

    def early(h, c):
        return max(0, min(2 * (c - h) + 1, units)) if 1 <= c < chunks - 1 else 0

    for c in range(chunks):
        acc[...] = jnp.zeros_like(acc)
        sq[...] = jnp.zeros_like(sq)

        def body(k, carry):
            j = c * steps + k
            slot = j % slots
            if c == 0:
                pattern_copy(k).wait()
            model_copy(j).wait()
            cols = pl.ds(pl.multiple_of(k * depth, depth), depth)
            block = mbuf[slot]
            acc[...] += jnp.dot(pat_v[:, cols], block, preferred_element_type=F32)
            wide = block.astype(F32)
            sq[...] += jnp.sum(wide * wide, axis=0, keepdims=True)

            @pl.when(j + slots < total_steps)
            def _():
                model_copy(j + slots).start()
            return carry

        lax.fori_loop(0, steps, body, 0)
        if c == 0:
            sib_copy.start()
        for d in range(2):
            rows = pl.ds(d * half_rows, half_rows)
            phi = phi_ref[rows, 0:1]
            part[d, c] = beta * (phi * acc[rows] - (0.5 * phi * phi) * sq[...])

            @pl.when(hops[d] == 0)
            def _():
                rs_copy(d, 2 * c).start()
                rs_copy(d, 2 * c + 1).start()

        for h in range(1, last):
            for u in range(early(h, c - 1), early(h, c)):
                for d in range(2):
                    @pl.when(hops[d] == h)
                    def _():
                        relay(d, u)

    done = [early(h, chunks - 2) for h in range(last)]
    for u in range(units):
        skipped = [h for h in range(1, last) if u < done[h]]
        for d in range(2):
            @pl.when(hops[d] > len(skipped))
            def _():
                relay(d, u)

    def weight_block(g, u):
        c, s = divmod(u, 2)
        return pl.ds((1 - g) * half_rows + s * sub, sub), pl.ds(c * width, width)

    def agz_copy(g, u):
        if u < units:
            rows, cols = weight_block(g, u)
            ref = w_ref.at[0, rows, cols]
        else:
            ref = dpart.at[0, g]
        return pltpu.make_async_remote_copy(
            src_ref=ref, dst_ref=ref, send_sem=agz_send.at[g, u], recv_sem=agz_recv.at[g, u],
            device_id={"pix": nexts[g]}, device_id_type=MESH)

    def ags_copy(g, u):
        if u < units:
            rows, cols = weight_block(g, u)
            src, dst = w_ref.at[0, rows, cols], w_ref.at[1, rows, cols]
        else:
            src, dst = dpart.at[0, g], dpart.at[1, g]
        return pltpu.make_async_remote_copy(
            src_ref=src, dst_ref=dst, send_sem=ags_send.at[g, u], recv_sem=ags_recv.at[g, u],
            device_id={"pat": 1 - core}, device_id_type=MESH)

    def st_copy(k):
        return pltpu.make_async_remote_copy(
            src_ref=st.at[0], dst_ref=st.at[k], send_sem=st_send.at[k], recv_sem=st_recv.at[k],
            device_id={"ori": lax.rem(ori + k, n_ori)}, device_id_type=MESH)

    for g in range(2):
        @pl.when(hops[g] == 0)
        def _():
            top = jnp.max(sc[...], axis=1, keepdims=True)
            total = jnp.sum(jnp.exp(sc[...] - top), axis=1, keepdims=True)
            lane = lax.broadcasted_iota(jnp.int32, (half_rows, 128), 1)
            packed = jnp.where(lane == 0, top, jnp.where(lane == 1, total, 0.0))
            st[0] = packed.T[0:8, :]
            for k in range(1, n_ori):
                st_copy(k).start()
            tops, totals = [top], [total]
            for k in range(1, n_ori):
                st_copy(k).wait_recv()
                other = jnp.concatenate(
                    [st[k], jnp.zeros((120, half_rows), F32)], axis=0).T
                tops.append(other[:, 0:1])
                totals.append(other[:, 1:2])
            most = functools.reduce(jnp.maximum, tops)
            whole = sum(t * jnp.exp(m - most) for m, t in zip(tops, totals))
            lse = most + jnp.log(whole)
            phi = phi_ref[(1 - g) * half_rows:(2 - g) * half_rows, 0:1]
            for c in range(chunks):
                cols = slice(c * width, (c + 1) * width)
                prob = jnp.exp(sc[:, cols] - lse)
                w_ref[0, (1 - g) * half_rows:(2 - g) * half_rows, cols] = (prob * phi).astype(BF16)
                dpart[0, g, :, cols] = jnp.sum(prob * (phi * phi), axis=0, keepdims=True)
                for u in (2 * c, 2 * c + 1):
                    agz_copy(g, u).start()
                    ags_copy(g, u).start()
            agz_copy(g, units).start()
            ags_copy(g, units).start()
            for k in range(1, n_ori):
                st_copy(k).wait_send()

    for u in range(units + 1):
        for g in range(2):
            @pl.when(hops[g] > 0)
            def _():
                agz_copy(g, u).wait_recv()

                @pl.when(hops[g] < last)
                def _():
                    agz_copy(g, u).start()
                ags_copy(g, u).start()

    for u in range(units + 1):
        for g in range(2):
            ags_copy(g, u).wait_recv()
    den_ref[...] = prior_weight + (
        (dpart[0, 0] + dpart[0, 1]) + (dpart[1, 0] + dpart[1, 1]))

    sib_copy.wait_recv()
    sib_copy.wait_send()
    for g in range(2):
        for u in range(units + 1):
            ags_copy(g, u).wait_send()

        @pl.when(hops[g] < last)
        def _():
            for u in range(units):
                rs_copy(g, u).wait_send()
            for u in range(units + 1):
                agz_copy(g, u).wait_send()


def update_kernel(half_ref, own_ref, sib_ref, w_ref, den_ref, model_ref, out_ref):
    dims = (((0,), (0,)), ((), ()))
    numer = lax.dot_general(own_ref[...], w_ref[0], dims, preferred_element_type=F32)
    numer += lax.dot_general(sib_ref[...], w_ref[1], dims, preferred_element_type=F32)
    numer += prior_weight * model_ref[...].astype(F32)
    out_ref[...] = (numer / den_ref[...]).astype(BF16)


def local(n_pix, n_ori, patterns, model, scale_table, scale_index, weight_table, weight_class):
    rows, pixels = patterns.shape
    columns = model.shape[1]
    half_pix = pixels // 2
    phi = jnp.broadcast_to(table_lookup(scale_table, scale_index)[:, None], (rows, 128))
    logw = table_lookup(weight_table, weight_class)[None, :]
    beta = float(pixels * n_pix) ** (-0.5)
    width = block_of(columns, 256)
    chunks = columns // width
    depth = block_of(pixels, 2048)
    steps = pixels // depth
    slots = min(8, chunks * steps)
    half_rows = rows // 2
    units = chunks * 2
    dma = pltpu.SemaphoreType.DMA
    any_spec = pl.BlockSpec(memory_space=pl.ANY)
    vmem_spec = pl.BlockSpec(memory_space=pltpu.VMEM)
    weights, den, sibling = pl.pallas_call(
        functools.partial(score_kernel, n_pix, n_ori, beta, chunks, width, steps, depth, slots),
        out_shape=(
            jax.ShapeDtypeStruct((2, rows, columns), BF16),
            jax.ShapeDtypeStruct((1, columns), F32),
            jax.ShapeDtypeStruct((rows, half_pix), BF16),
        ),
        in_specs=[any_spec, any_spec, vmem_spec, vmem_spec],
        out_specs=(vmem_spec, vmem_spec, any_spec),
        scratch_shapes=[
            pltpu.VMEM((rows, pixels), BF16),
            pltpu.VMEM((slots, depth, width), BF16),
            pltpu.VMEM((rows, width), F32),
            pltpu.VMEM((1, width), F32),
            pltpu.VMEM((2, chunks, half_rows, width), F32),
            pltpu.VMEM((2, chunks, half_rows, width), F32),
            pltpu.VMEM((half_rows, columns), F32),
            pltpu.VMEM((n_ori, 8, half_rows), F32),
            pltpu.VMEM((2, 2, 1, columns), F32),
            dma((steps,)),
            dma((slots,)),
            dma((2,)),
            dma((2, units)),
            dma((2, units)),
            dma((n_ori,)),
            dma((n_ori,)),
            dma((2, units + 1)),
            dma((2, units + 1)),
            dma((2, units + 1)),
            dma((2, units + 1)),
        ],
        compiler_params=pltpu.CompilerParams(
            collective_id=0, has_side_effects=True, vmem_limit_bytes=56 * 2**20),
        cost_estimate=pl.CostEstimate(
            flops=2 * rows * pixels * columns,
            bytes_accessed=2 * pixels * (rows + columns), transcendentals=rows * columns),
    )(patterns, model, phi, logw)

    block = block_of(half_pix, 512)
    blocks = half_pix // block
    own_half = lax.axis_index("pat").astype(jnp.int32).reshape(1)
    return pl.pallas_call(
        update_kernel,
        out_shape=jax.ShapeDtypeStruct((half_pix, columns), BF16),
        grid_spec=pltpu.PrefetchScalarGridSpec(
            num_scalar_prefetch=1,
            grid=(blocks,),
            in_specs=[
                pl.BlockSpec((rows, block), lambda i, half: (0, half[0] * blocks + i)),
                pl.BlockSpec((rows, block), lambda i, half: (0, i)),
                pl.BlockSpec((2, rows, columns), lambda i, half: (0, 0, 0)),
                pl.BlockSpec((1, columns), lambda i, half: (0, 0)),
                pl.BlockSpec((block, columns), lambda i, half: (half[0] * blocks + i, 0)),
            ],
            out_specs=pl.BlockSpec((block, columns), lambda i, half: (i, 0)),
        ),
        compiler_params=pltpu.CompilerParams(vmem_limit_bytes=48 * 2**20),
        cost_estimate=pl.CostEstimate(
            flops=4 * rows * half_pix * columns,
            bytes_accessed=4 * half_pix * (rows + columns), transcendentals=0),
    )(own_half, patterns, sibling, weights, den, model)


def solution(mesh):
    placed = (
        P(("grp", "pat"), "pix"),
        P(("grp", "pix"), "ori"),
        P("grp"),
        P(("grp", "pat")),
        P("grp"),
        P(("grp", "ori")),
    )
    return jax.shard_map(
        functools.partial(local, mesh.shape["pix"], mesh.shape["ori"]),
        mesh=mesh,
        in_specs=placed,
        out_specs=P(("grp", "pix", "pat"), "ori"),
        check_vma=False,
    )
```

```python
import functools

import jax
import jax.numpy as jnp
from jax import lax
from jax.experimental import pallas as pl
from jax.experimental.pallas import tpu as pltpu
from jax.sharding import PartitionSpec as P

prior_weight = 0.5
MESH = pl.DeviceIdType.MESH
F32 = jnp.float32
BF16 = jnp.bfloat16


def table_lookup(table, index):
    levels = jnp.arange(table.shape[0], dtype=jnp.int32)
    return jnp.sum(jnp.where(index[:, None] == levels[None, :], table[None, :], 0.0), axis=1)


def block_of(size, most):
    block = min(size, most)
    while size % block:
        block //= 2
    return block


def score_kernel(
    n_pix, n_ori, beta, chunks, subs, width, steps, depth, slots,
    pat_hbm, model_hbm, phi_ref, logw_ref,
    w_ref, den_ref, sib_ref,
    pat_v, mbuf, acc, sq, part, rx, sc, st, dpart,
    pat_sem, m_sem, sib_sem, rs_send, rs_recv, st_send, st_recv,
    agz_send, agz_recv, ags_send, ags_recv,
):
    z = lax.axis_index("pix")
    core = lax.axis_index("pat")
    ori = lax.axis_index("ori")
    last = n_pix - 1
    half_rows = part.shape[2]
    sub = half_rows // subs
    units = chunks * subs
    hops = (z, last - z)
    nexts = (lax.rem(z + 1, n_pix), lax.rem(z + n_pix - 1, n_pix))

    def model_copy(j):
        c, k = j // steps, j % steps
        return pltpu.make_async_copy(
            model_hbm.at[pl.ds(k * depth, depth), pl.ds(c * width, width)],
            mbuf.at[j % slots], m_sem.at[j % slots])

    def pattern_copy(k):
        cols = pl.ds(k * depth, depth)
        return pltpu.make_async_copy(pat_hbm.at[:, cols], pat_v.at[:, cols], pat_sem.at[k])

    total_steps = chunks * steps
    for k in range(steps):
        pattern_copy(k).start()
        if k < min(slots, total_steps):
            model_copy(k).start()
    for j in range(steps, min(slots, total_steps)):
        model_copy(j).start()

    barrier = pltpu.get_barrier_semaphore()
    for d in range(2):
        @pl.when(hops[d] < last)
        def _():
            pl.semaphore_signal(barrier, inc=1, device_id={"pix": nexts[d]}, device_id_type=MESH)
    pl.semaphore_signal(barrier, inc=1, device_id={"pat": 1 - core}, device_id_type=MESH)
    for k in range(1, n_ori):
        pl.semaphore_signal(
            barrier, inc=1, device_id={"ori": lax.rem(ori + k, n_ori)}, device_id_type=MESH)
    @pl.when(hops[0] * hops[1] == 0)
    def _():
        pl.semaphore_wait(barrier, n_ori + 1)

    @pl.when(hops[0] * hops[1] > 0)
    def _():
        pl.semaphore_wait(barrier, n_ori + 2)

    half_pix = sib_ref.shape[1]
    piece = sib_ref.shape[0] // total_steps

    def sib_copy(j):
        rows = pl.ds(pl.multiple_of(j * piece, piece), piece)
        return pltpu.make_async_remote_copy(
            src_ref=pat_hbm.at[rows, pl.ds((1 - core) * half_pix, half_pix)],
            dst_ref=sib_ref.at[rows],
            send_sem=sib_sem.at[0, j], recv_sem=sib_sem.at[1, j],
            device_id={"pat": 1 - core}, device_id_type=MESH)

    def rows_of(s):
        return pl.ds(s * sub, sub)

    def rs_copy(d, u):
        c, s = divmod(u, subs)
        return pltpu.make_async_remote_copy(
            src_ref=part.at[d, c, rows_of(s)], dst_ref=rx.at[d, c, rows_of(s)],
            send_sem=rs_send.at[d, u], recv_sem=rs_recv.at[d, u],
            device_id={"pix": nexts[d]}, device_id_type=MESH)

    def relay(d, u):
        c, s = divmod(u, subs)
        rs_copy(d, u).wait_recv()
        rows = rows_of(s)

        @pl.when(hops[d] < last)
        def _():
            part[d, c, rows] = part[d, c, rows] + rx[d, c, rows]
            rs_copy(d, u).start()

        @pl.when(hops[d] == last)
        def _():
            cols = pl.ds(c * width, width)
            sc[rows, cols] = part[d, c, rows] + rx[d, c, rows] + logw_ref[:, cols]

    marks = []
    if chunks > 1 and steps >= 8 and last > 2 and subs > 1:
        marks = [(steps // 2, ((1, 0),)), (steps - 1, ((1, 1), (2, 0)))]
    relayed = {pair for _, pairs in marks for pair in pairs}

    for c in range(chunks):
        acc[...] = jnp.zeros_like(acc)
        sq[...] = jnp.zeros_like(sq)

        def body(k, carry):
            j = c * steps + k
            slot = j % slots
            if c == 0:
                pattern_copy(k).wait()
            model_copy(j).wait()
            cols = pl.ds(pl.multiple_of(k * depth, depth), depth)
            block = mbuf[slot]
            acc[...] += jnp.dot(pat_v[:, cols], block, preferred_element_type=F32)
            wide = block.astype(F32)
            sq[...] += jnp.sum(wide * wide, axis=0, keepdims=True)

            @pl.when(j + slots < total_steps)
            def _():
                model_copy(j + slots).start()
            sib_copy(j).start()
            return carry

        start = 0
        for stop, pairs in (marks if c == chunks - 1 else []) + [(steps, ())]:
            lax.fori_loop(start, stop, body, 0)
            start = stop
            for h, u in pairs:
                for d in range(2):
                    @pl.when(hops[d] == h)
                    def _():
                        relay(d, u)
        for d in range(2):
            rows = pl.ds(d * half_rows, half_rows)
            phi = phi_ref[rows, 0:1]
            part[d, c] = beta * (phi * acc[rows] - (0.5 * phi * phi) * sq[...])

            @pl.when(hops[d] == 0)
            def _():
                for u in range(c * subs, (c + 1) * subs):
                    rs_copy(d, u).start()

    for u in range(units):
        skipped = sum((h, u) in relayed for h in range(1, last))
        for d in range(2):
            @pl.when(hops[d] > skipped)
            def _():
                relay(d, u)

    def weight_block(g, u):
        c, s = divmod(u, subs)
        return pl.ds((1 - g) * half_rows + s * sub, sub), pl.ds(c * width, width)

    def agz_copy(g, u):
        if u < units:
            rows, cols = weight_block(g, u)
            ref = w_ref.at[0, rows, cols]
        else:
            ref = dpart.at[0, g]
        return pltpu.make_async_remote_copy(
            src_ref=ref, dst_ref=ref, send_sem=agz_send.at[g, u], recv_sem=agz_recv.at[g, u],
            device_id={"pix": nexts[g]}, device_id_type=MESH)

    def ags_copy(g, u):
        if u < units:
            rows, cols = weight_block(g, u)
            src, dst = w_ref.at[0, rows, cols], w_ref.at[1, rows, cols]
        else:
            src, dst = dpart.at[0, g], dpart.at[1, g]
        return pltpu.make_async_remote_copy(
            src_ref=src, dst_ref=dst, send_sem=ags_send.at[g, u], recv_sem=ags_recv.at[g, u],
            device_id={"pat": 1 - core}, device_id_type=MESH)

    def st_copy(k):
        return pltpu.make_async_remote_copy(
            src_ref=st.at[0], dst_ref=st.at[k], send_sem=st_send.at[k], recv_sem=st_recv.at[k],
            device_id={"ori": lax.rem(ori + k, n_ori)}, device_id_type=MESH)

    for g in range(2):
        @pl.when(hops[g] == 0)
        def _():
            top = jnp.max(sc[...], axis=1, keepdims=True)
            total = jnp.sum(jnp.exp(sc[...] - top), axis=1, keepdims=True)
            lane = lax.broadcasted_iota(jnp.int32, (half_rows, 128), 1)
            packed = jnp.where(lane == 0, top, jnp.where(lane == 1, total, 0.0))
            st[0] = packed.T[0:8, :]
            for k in range(1, n_ori):
                st_copy(k).start()
            tops, totals = [top], [total]
            for k in range(1, n_ori):
                st_copy(k).wait_recv()
                other = jnp.concatenate(
                    [st[k], jnp.zeros((120, half_rows), F32)], axis=0).T
                tops.append(other[:, 0:1])
                totals.append(other[:, 1:2])
            most = functools.reduce(jnp.maximum, tops)
            whole = sum(t * jnp.exp(m - most) for m, t in zip(tops, totals))
            lse = most + jnp.log(whole)
            phi = phi_ref[(1 - g) * half_rows:(2 - g) * half_rows, 0:1]
            for c in range(chunks):
                cols = slice(c * width, (c + 1) * width)
                prob = jnp.exp(sc[:, cols] - lse)
                w_ref[0, (1 - g) * half_rows:(2 - g) * half_rows, cols] = (prob * phi).astype(BF16)
                dpart[0, g, :, cols] = jnp.sum(prob * (phi * phi), axis=0, keepdims=True)
                for u in range(c * subs, (c + 1) * subs):
                    agz_copy(g, u).start()
                    ags_copy(g, u).start()
            agz_copy(g, units).start()
            ags_copy(g, units).start()
            for k in range(1, n_ori):
                st_copy(k).wait_send()

    for u in range(units + 1):
        for g in range(2):
            @pl.when(hops[g] > 0)
            def _():
                agz_copy(g, u).wait_recv()

                @pl.when(hops[g] < last)
                def _():
                    agz_copy(g, u).start()
                ags_copy(g, u).start()

    for u in range(units + 1):
        for g in range(2):
            ags_copy(g, u).wait_recv()
    den_ref[...] = 1.0 / (prior_weight + (
        (dpart[0, 0] + dpart[0, 1]) + (dpart[1, 0] + dpart[1, 1])))

    def settle(j, carry):
        sib_copy(j).wait_recv()
        sib_copy(j).wait_send()
        return carry

    lax.fori_loop(0, total_steps, settle, 0)
    for g in range(2):
        for u in range(units + 1):
            ags_copy(g, u).wait_send()

        @pl.when(hops[g] < last)
        def _():
            for u in range(units):
                rs_copy(g, u).wait_send()
            for u in range(units + 1):
                agz_copy(g, u).wait_send()


def update_kernel(width, half_ref, own_ref, sib_ref, w_ref, inverse_ref, model_ref, out_ref):
    pats = jnp.concatenate([own_ref[...].T, sib_ref[...].T], axis=1)
    both, rows, columns = w_ref.shape
    for c in range(columns // width):
        cols = slice(c * width, (c + 1) * width)
        weights = w_ref[:, :, cols].reshape(both * rows, width)
        numer = jnp.dot(pats, weights, preferred_element_type=F32)
        numer += prior_weight * model_ref[:, cols].astype(F32)
        out_ref[:, cols] = (numer * inverse_ref[:, cols]).astype(BF16)


def local(n_pix, n_ori, patterns, model, scale_table, scale_index, weight_table, weight_class):
    rows, pixels = patterns.shape
    columns = model.shape[1]
    half_pix = pixels // 2
    phi = jnp.broadcast_to(table_lookup(scale_table, scale_index)[:, None], (rows, 128))
    logw = table_lookup(weight_table, weight_class)[None, :]
    beta = float(pixels * n_pix) ** (-0.5)
    width = block_of(columns, 512)
    chunks = columns // width
    depth = block_of(pixels, 2048)
    steps = pixels // depth
    slots = min(8, chunks * steps)
    half_rows = rows // 2
    subs = 4
    units = chunks * subs
    dma = pltpu.SemaphoreType.DMA
    any_spec = pl.BlockSpec(memory_space=pl.ANY)
    vmem_spec = pl.BlockSpec(memory_space=pltpu.VMEM)
    weights, inverse, sibling = pl.pallas_call(
        functools.partial(score_kernel, n_pix, n_ori, beta, chunks, subs, width, steps, depth, slots),
        out_shape=(
            jax.ShapeDtypeStruct((2, rows, columns), BF16),
            jax.ShapeDtypeStruct((1, columns), F32),
            jax.ShapeDtypeStruct((rows, half_pix), BF16),
        ),
        in_specs=[any_spec, any_spec, vmem_spec, vmem_spec],
        out_specs=(vmem_spec, vmem_spec, any_spec),
        scratch_shapes=[
            pltpu.VMEM((rows, pixels), BF16),
            pltpu.VMEM((slots, depth, width), BF16),
            pltpu.VMEM((rows, width), F32),
            pltpu.VMEM((1, width), F32),
            pltpu.VMEM((2, chunks, half_rows, width), F32),
            pltpu.VMEM((2, chunks, half_rows, width), F32),
            pltpu.VMEM((half_rows, columns), F32),
            pltpu.VMEM((n_ori, 8, half_rows), F32),
            pltpu.VMEM((2, 2, 1, columns), F32),
            dma((steps,)),
            dma((slots,)),
            dma((2, chunks * steps)),
            dma((2, units)),
            dma((2, units)),
            dma((n_ori,)),
            dma((n_ori,)),
            dma((2, units + 1)),
            dma((2, units + 1)),
            dma((2, units + 1)),
            dma((2, units + 1)),
        ],
        compiler_params=pltpu.CompilerParams(
            collective_id=0, has_side_effects=True, vmem_limit_bytes=56 * 2**20),
        cost_estimate=pl.CostEstimate(
            flops=2 * rows * pixels * columns,
            bytes_accessed=2 * pixels * (rows + columns), transcendentals=rows * columns),
    )(patterns, model, phi, logw)

    block = block_of(half_pix, 512)
    blocks = half_pix // block
    own_half = lax.axis_index("pat").astype(jnp.int32).reshape(1)
    return pl.pallas_call(
        functools.partial(update_kernel, block_of(columns, 256)),
        out_shape=jax.ShapeDtypeStruct((half_pix, columns), BF16),
        grid_spec=pltpu.PrefetchScalarGridSpec(
            num_scalar_prefetch=1,
            grid=(blocks,),
            in_specs=[
                pl.BlockSpec((rows, block), lambda i, half: (0, half[0] * blocks + i)),
                pl.BlockSpec((rows, block), lambda i, half: (0, i)),
                pl.BlockSpec((2, rows, columns), lambda i, half: (0, 0, 0)),
                pl.BlockSpec((1, columns), lambda i, half: (0, 0)),
                pl.BlockSpec((block, columns), lambda i, half: (half[0] * blocks + i, 0)),
            ],
            out_specs=pl.BlockSpec((block, columns), lambda i, half: (i, 0)),
        ),
        compiler_params=pltpu.CompilerParams(vmem_limit_bytes=60 * 2**20),
        cost_estimate=pl.CostEstimate(
            flops=4 * rows * half_pix * columns,
            bytes_accessed=4 * half_pix * (rows + columns), transcendentals=0),
    )(own_half, patterns, sibling, weights, inverse, model)


def solution(mesh):
    placed = (
        P(("grp", "pat"), "pix"),
        P(("grp", "pix"), "ori"),
        P("grp"),
        P(("grp", "pat")),
        P("grp"),
        P(("grp", "ori")),
    )
    return jax.shard_map(
        functools.partial(local, mesh.shape["pix"], mesh.shape["ori"]),
        mesh=mesh,
        in_specs=placed,
        out_specs=P(("grp", "pix", "pat"), "ori"),
        check_vma=False,
    )
```

```python
import functools

import jax
import jax.numpy as jnp
from jax import lax
from jax.experimental import pallas as pl
from jax.experimental.pallas import tpu as pltpu
from jax.sharding import PartitionSpec as P

prior_weight = 0.5
MESH = pl.DeviceIdType.MESH
F32 = jnp.float32
BF16 = jnp.bfloat16


def table_lookup(table, index):
    levels = jnp.arange(table.shape[0], dtype=jnp.int32)
    return jnp.sum(jnp.where(index[:, None] == levels[None, :], table[None, :], 0.0), axis=1)


def block_of(size, most):
    block = min(size, most)
    while size % block:
        block //= 2
    return block


def score_kernel(
    n_pix, n_ori, beta, chunks, subs, width, steps, depth, slots,
    pat_hbm, model_hbm, phi_ref, logw_ref,
    w_ref, den_ref,
    pat_v, mbuf, acc, sq, part, rx, sc, st, dpart,
    pat_sem, m_sem, rs_send, rs_recv, st_send, st_recv,
    agz_send, agz_recv, ags_send, ags_recv,
):
    z = lax.axis_index("pix")
    core = lax.axis_index("pat")
    ori = lax.axis_index("ori")
    last = n_pix - 1
    half_rows = part.shape[2]
    sub = half_rows // subs
    units = chunks * subs
    hops = (z, last - z)
    nexts = (lax.rem(z + 1, n_pix), lax.rem(z + n_pix - 1, n_pix))

    def model_copy(j):
        c, k = j // steps, j % steps
        return pltpu.make_async_copy(
            model_hbm.at[pl.ds(k * depth, depth), pl.ds(c * width, width)],
            mbuf.at[j % slots], m_sem.at[j % slots])

    def pattern_copy(k):
        cols = pl.ds(k * depth, depth)
        return pltpu.make_async_copy(pat_hbm.at[:, cols], pat_v.at[:, cols], pat_sem.at[k])

    total_steps = chunks * steps
    fine = block_of(depth, 512)
    for k in range(steps):
        pattern_copy(k).start()
        if k < min(slots, total_steps):
            model_copy(k).start()
    for j in range(steps, min(slots, total_steps)):
        model_copy(j).start()

    barrier = pltpu.get_barrier_semaphore()
    for d in range(2):
        @pl.when(hops[d] < last)
        def _():
            pl.semaphore_signal(barrier, inc=1, device_id={"pix": nexts[d]}, device_id_type=MESH)
    pl.semaphore_signal(barrier, inc=1, device_id={"pat": 1 - core}, device_id_type=MESH)
    for k in range(1, n_ori):
        pl.semaphore_signal(
            barrier, inc=1, device_id={"ori": lax.rem(ori + k, n_ori)}, device_id_type=MESH)
    @pl.when(hops[0] * hops[1] == 0)
    def _():
        pl.semaphore_wait(barrier, n_ori + 1)

    @pl.when(hops[0] * hops[1] > 0)
    def _():
        pl.semaphore_wait(barrier, n_ori + 2)

    def rows_of(s):
        return pl.ds(s * sub, sub)

    def rs_copy(d, u):
        c, s = divmod(u, subs)
        return pltpu.make_async_remote_copy(
            src_ref=part.at[d, c, rows_of(s)], dst_ref=rx.at[d, c, rows_of(s)],
            send_sem=rs_send.at[d, u], recv_sem=rs_recv.at[d, u],
            device_id={"pix": nexts[d]}, device_id_type=MESH)

    def relay(d, u):
        c, s = divmod(u, subs)
        rs_copy(d, u).wait_recv()
        rows = rows_of(s)

        @pl.when(hops[d] < last)
        def _():
            part[d, c, rows] = part[d, c, rows] + rx[d, c, rows]
            rs_copy(d, u).start()

        @pl.when(hops[d] == last)
        def _():
            cols = pl.ds(c * width, width)
            sc[rows, cols] = part[d, c, rows] + rx[d, c, rows] + logw_ref[:, cols]

    marks = []
    if chunks > 1 and steps >= 8 and last > 2 and subs > 1:
        marks = [(steps // 2, ((1, 0),)), (steps - 1, ((1, 1), (2, 0)))]
    relayed = {pair for _, pairs in marks for pair in pairs}

    for c in range(chunks):
        acc[...] = jnp.zeros_like(acc)
        sq[...] = jnp.zeros_like(sq)

        def body(k, carry):
            j = c * steps + k
            slot = j % slots
            if c == 0:
                pattern_copy(k).wait()
            model_copy(j).wait()
            def inner(i, carry):
                cols = pl.ds(pl.multiple_of(k * depth + i * fine, fine), fine)
                block = mbuf[slot, pl.ds(pl.multiple_of(i * fine, fine), fine)]
                acc[...] += jnp.dot(pat_v[:, cols], block, preferred_element_type=F32)
                wide = block.astype(F32).reshape(fine // 8, 8, width)
                sq[...] += jnp.sum(wide * wide, axis=0)
                return carry

            lax.fori_loop(0, depth // fine, inner, 0)

            @pl.when(j + slots < total_steps)
            def _():
                model_copy(j + slots).start()
            return carry

        start = 0
        for stop, pairs in (marks if c == chunks - 1 else []) + [(steps, ())]:
            lax.fori_loop(start, stop, body, 0)
            start = stop
            for h, u in pairs:
                for d in range(2):
                    @pl.when(hops[d] == h)
                    def _():
                        relay(d, u)
        squares = jnp.sum(sq[...], axis=0, keepdims=True)
        for d in range(2):
            rows = pl.ds(d * half_rows, half_rows)
            phi = phi_ref[rows, 0:1]
            part[d, c] = beta * (phi * acc[rows] - (0.5 * phi * phi) * squares)

            @pl.when(hops[d] == 0)
            def _():
                for u in range(c * subs, (c + 1) * subs):
                    rs_copy(d, u).start()

    for u in range(units):
        skipped = sum((h, u) in relayed for h in range(1, last))
        for d in range(2):
            @pl.when(hops[d] > skipped)
            def _():
                relay(d, u)

    def weight_block(g, u):
        c, s = divmod(u, subs)
        return pl.ds((1 - g) * half_rows + s * sub, sub), pl.ds(c * width, width)

    def agz_copy(g, u):
        if u < units:
            rows, cols = weight_block(g, u)
            ref = w_ref.at[0, rows, cols]
        else:
            ref = dpart.at[0, g]
        return pltpu.make_async_remote_copy(
            src_ref=ref, dst_ref=ref, send_sem=agz_send.at[g, u], recv_sem=agz_recv.at[g, u],
            device_id={"pix": nexts[g]}, device_id_type=MESH)

    def ags_copy(g, u):
        if u < units:
            rows, cols = weight_block(g, u)
            src, dst = w_ref.at[0, rows, cols], w_ref.at[1, rows, cols]
        else:
            src, dst = dpart.at[0, g], dpart.at[1, g]
        return pltpu.make_async_remote_copy(
            src_ref=src, dst_ref=dst, send_sem=ags_send.at[g, u], recv_sem=ags_recv.at[g, u],
            device_id={"pat": 1 - core}, device_id_type=MESH)

    def st_copy(k):
        return pltpu.make_async_remote_copy(
            src_ref=st.at[0], dst_ref=st.at[k], send_sem=st_send.at[k], recv_sem=st_recv.at[k],
            device_id={"ori": lax.rem(ori + k, n_ori)}, device_id_type=MESH)

    for g in range(2):
        @pl.when(hops[g] == 0)
        def _():
            top = jnp.max(sc[...], axis=1, keepdims=True)
            total = jnp.sum(jnp.exp(sc[...] - top), axis=1, keepdims=True)
            lane = lax.broadcasted_iota(jnp.int32, (half_rows, 128), 1)
            packed = jnp.where(lane == 0, top, jnp.where(lane == 1, total, 0.0))
            st[0] = packed.T[0:8, :]
            for k in range(1, n_ori):
                st_copy(k).start()
            tops, totals = [top], [total]
            for k in range(1, n_ori):
                st_copy(k).wait_recv()
                other = jnp.concatenate(
                    [st[k], jnp.zeros((120, half_rows), F32)], axis=0).T
                tops.append(other[:, 0:1])
                totals.append(other[:, 1:2])
            most = functools.reduce(jnp.maximum, tops)
            whole = sum(t * jnp.exp(m - most) for m, t in zip(tops, totals))
            lse = most + jnp.log(whole)
            phi = phi_ref[(1 - g) * half_rows:(2 - g) * half_rows, 0:1]
            for c in range(chunks):
                cols = slice(c * width, (c + 1) * width)
                prob = jnp.exp(sc[:, cols] - lse)
                w_ref[0, (1 - g) * half_rows:(2 - g) * half_rows, cols] = (prob * phi).astype(BF16)
                dpart[0, g, :, cols] = jnp.sum(prob * (phi * phi), axis=0, keepdims=True)
                for u in range(c * subs, (c + 1) * subs):
                    agz_copy(g, u).start()
                    ags_copy(g, u).start()
            agz_copy(g, units).start()
            ags_copy(g, units).start()
            for k in range(1, n_ori):
                st_copy(k).wait_send()

    for u in range(units + 1):
        for g in range(2):
            @pl.when(hops[g] > 0)
            def _():
                agz_copy(g, u).wait_recv()

                @pl.when(hops[g] < last)
                def _():
                    agz_copy(g, u).start()
                ags_copy(g, u).start()

    for u in range(units + 1):
        for g in range(2):
            ags_copy(g, u).wait_recv()
    den_ref[...] = 1.0 / (prior_weight + (
        (dpart[0, 0] + dpart[0, 1]) + (dpart[1, 0] + dpart[1, 1])))

    for g in range(2):
        for u in range(units + 1):
            ags_copy(g, u).wait_send()

        @pl.when(hops[g] < last)
        def _():
            for u in range(units):
                rs_copy(g, u).wait_send()
            for u in range(units + 1):
                agz_copy(g, u).wait_send()


def update_kernel(width, place_ref, pat_ref, first_ref, second_ref, inverse_ref, model_ref, out_ref):
    pats = pat_ref[...].T
    columns = out_ref.shape[1]
    for c in range(columns // width):
        cols = slice(c * width, (c + 1) * width)
        weights = jnp.concatenate([first_ref[0, :, cols], second_ref[0, :, cols]], axis=0)
        numer = jnp.dot(pats, weights, preferred_element_type=F32)
        numer += prior_weight * model_ref[:, cols].astype(F32)
        out_ref[:, cols] = (numer * inverse_ref[:, cols]).astype(BF16)


def local(n_pix, n_ori, patterns, model, scale_table, scale_index, weight_table, weight_class):
    rows, pixels = patterns.shape
    columns = model.shape[1]
    half_pix = pixels // 2
    phi = jnp.broadcast_to(table_lookup(scale_table, scale_index)[:, None], (rows, 128))
    logw = table_lookup(weight_table, weight_class)[None, :]
    beta = float(pixels * n_pix) ** (-0.5)
    width = block_of(columns, 512)
    chunks = columns // width
    depth = block_of(pixels, 2048)
    steps = pixels // depth
    slots = min(8, chunks * steps)
    half_rows = rows // 2
    subs = 4
    units = chunks * subs
    dma = pltpu.SemaphoreType.DMA
    any_spec = pl.BlockSpec(memory_space=pl.ANY)
    vmem_spec = pl.BlockSpec(memory_space=pltpu.VMEM)
    gathered = lax.all_gather(patterns, "pat", axis=0, tiled=True)
    weights, inverse = pl.pallas_call(
        functools.partial(score_kernel, n_pix, n_ori, beta, chunks, subs, width, steps, depth, slots),
        out_shape=(
            jax.ShapeDtypeStruct((2, rows, columns), BF16),
            jax.ShapeDtypeStruct((1, columns), F32),
        ),
        in_specs=[any_spec, any_spec, vmem_spec, vmem_spec],
        out_specs=(vmem_spec, vmem_spec),
        scratch_shapes=[
            pltpu.VMEM((rows, pixels), BF16),
            pltpu.VMEM((slots, depth, width), BF16),
            pltpu.VMEM((rows, width), F32),
            pltpu.VMEM((8, width), F32),
            pltpu.VMEM((2, chunks, half_rows, width), F32),
            pltpu.VMEM((2, chunks, half_rows, width), F32),
            pltpu.VMEM((half_rows, columns), F32),
            pltpu.VMEM((n_ori, 8, half_rows), F32),
            pltpu.VMEM((2, 2, 1, columns), F32),
            dma((steps,)),
            dma((slots,)),
            dma((2, units)),
            dma((2, units)),
            dma((n_ori,)),
            dma((n_ori,)),
            dma((2, units + 1)),
            dma((2, units + 1)),
            dma((2, units + 1)),
            dma((2, units + 1)),
        ],
        compiler_params=pltpu.CompilerParams(
            collective_id=0, has_side_effects=True, vmem_limit_bytes=56 * 2**20),
        cost_estimate=pl.CostEstimate(
            flops=2 * rows * pixels * columns,
            bytes_accessed=2 * pixels * (rows + columns), transcendentals=rows * columns),
    )(patterns, model, phi, logw)

    block = block_of(half_pix, 512)
    blocks = half_pix // block
    own_half = lax.axis_index("pat").astype(jnp.int32).reshape(1)
    return pl.pallas_call(
        functools.partial(update_kernel, block_of(columns, 256)),
        out_shape=jax.ShapeDtypeStruct((half_pix, columns), BF16),
        grid_spec=pltpu.PrefetchScalarGridSpec(
            num_scalar_prefetch=1,
            grid=(blocks,),
            in_specs=[
                pl.BlockSpec((2 * rows, block), lambda i, half: (0, half[0] * blocks + i)),
                pl.BlockSpec((1, rows, columns), lambda i, half: (half[0], 0, 0)),
                pl.BlockSpec((1, rows, columns), lambda i, half: (1 - half[0], 0, 0)),
                pl.BlockSpec((1, columns), lambda i, half: (0, 0)),
                pl.BlockSpec((block, columns), lambda i, half: (half[0] * blocks + i, 0)),
            ],
            out_specs=pl.BlockSpec((block, columns), lambda i, half: (i, 0)),
        ),
        compiler_params=pltpu.CompilerParams(vmem_limit_bytes=60 * 2**20),
        cost_estimate=pl.CostEstimate(
            flops=4 * rows * half_pix * columns,
            bytes_accessed=4 * half_pix * (rows + columns), transcendentals=0),
    )(own_half, gathered, weights, weights, inverse, model)


def solution(mesh):
    placed = (
        P(("grp", "pat"), "pix"),
        P(("grp", "pix"), "ori"),
        P("grp"),
        P(("grp", "pat")),
        P("grp"),
        P(("grp", "ori")),
    )
    return jax.shard_map(
        functools.partial(local, mesh.shape["pix"], mesh.shape["ori"]),
        mesh=mesh,
        in_specs=placed,
        out_specs=P(("grp", "pix", "pat"), "ori"),
        check_vma=False,
    )
```

```python
import functools

import jax
import jax.numpy as jnp
from jax import lax
from jax.experimental import pallas as pl
from jax.experimental.pallas import tpu as pltpu
from jax.sharding import PartitionSpec as P

prior_weight = 0.5
MESH = pl.DeviceIdType.MESH
F32 = jnp.float32
BF16 = jnp.bfloat16


def table_lookup(table, index):
    levels = jnp.arange(table.shape[0], dtype=jnp.int32)
    return jnp.sum(jnp.where(index[:, None] == levels[None, :], table[None, :], 0.0), axis=1)


def block_of(size, most):
    block = min(size, most)
    while size % block:
        block //= 2
    return block


def score_kernel(
    n_pix, n_ori, beta, chunks, subs, width, steps, depth, slots,
    pat_hbm, model_hbm, phi_ref, logw_ref,
    w_ref, den_ref,
    pat_v, mbuf, acc, sq, part, rx, sc, st, dpart,
    pat_sem, m_sem, rs_send, rs_recv, st_send, st_recv,
    agz_send, agz_recv, ags_send, ags_recv,
):
    z = lax.axis_index("pix")
    core = lax.axis_index("pat")
    ori = lax.axis_index("ori")
    last = n_pix - 1
    half_rows = part.shape[2]
    sub = half_rows // subs
    units = chunks * subs
    hops = (z, last - z)
    nexts = (lax.rem(z + 1, n_pix), lax.rem(z + n_pix - 1, n_pix))

    def model_copy(j):
        c, k = j // steps, j % steps
        return pltpu.make_async_copy(
            model_hbm.at[pl.ds(k * depth, depth), pl.ds(c * width, width)],
            mbuf.at[j % slots], m_sem.at[j % slots])

    def pattern_copy(k):
        cols = pl.ds(k * depth, depth)
        return pltpu.make_async_copy(pat_hbm.at[:, cols], pat_v.at[:, cols], pat_sem.at[k])

    total_steps = chunks * steps
    fine = block_of(depth, 2048)
    for k in range(steps):
        pattern_copy(k).start()
        if k < min(slots, total_steps):
            model_copy(k).start()
    for j in range(steps, min(slots, total_steps)):
        model_copy(j).start()

    barrier = pltpu.get_barrier_semaphore()
    for d in range(2):
        @pl.when(hops[d] < last)
        def _():
            pl.semaphore_signal(barrier, inc=1, device_id={"pix": nexts[d]}, device_id_type=MESH)
    pl.semaphore_signal(barrier, inc=1, device_id={"pat": 1 - core}, device_id_type=MESH)
    for k in range(1, n_ori):
        pl.semaphore_signal(
            barrier, inc=1, device_id={"ori": lax.rem(ori + k, n_ori)}, device_id_type=MESH)
    @pl.when(hops[0] * hops[1] == 0)
    def _():
        pl.semaphore_wait(barrier, n_ori + 1)

    @pl.when(hops[0] * hops[1] > 0)
    def _():
        pl.semaphore_wait(barrier, n_ori + 2)

    def rows_of(s):
        return pl.ds(pl.multiple_of(s * sub, sub), sub)

    def rs_copy(d, u):
        c, s = u // subs, u % subs
        return pltpu.make_async_remote_copy(
            src_ref=part.at[d, c, rows_of(s)], dst_ref=rx.at[d, c, rows_of(s)],
            send_sem=rs_send.at[d, u], recv_sem=rs_recv.at[d, u],
            device_id={"pix": nexts[d]}, device_id_type=MESH)

    def relay(d, u):
        c, s = u // subs, u % subs
        rs_copy(d, u).wait_recv()
        rows = rows_of(s)

        @pl.when(hops[d] < last)
        def _():
            part[d, c, rows] = part[d, c, rows] + rx[d, c, rows]
            rs_copy(d, u).start()

        @pl.when(hops[d] == last)
        def _():
            cols = pl.ds(pl.multiple_of(c * width, width), width)
            sc[rows, cols] = part[d, c, rows] + rx[d, c, rows] + logw_ref[:, cols]

    def relay_slot(t):
        for d in range(2):
            u = t - 2 * (hops[d] - 1)

            @pl.when((hops[d] > 0) & (u >= 0) & (u < units))
            def _():
                relay(d, u)

    early = (chunks - 1) * subs
    if early > steps:
        early = 0

    for c in range(chunks):
        acc[...] = jnp.zeros_like(acc)
        sq[...] = jnp.zeros_like(sq)

        def body(k, carry):
            j = c * steps + k
            slot = j % slots
            if c == 0:
                pattern_copy(k).wait()
            model_copy(j).wait()
            def inner(i, carry):
                cols = pl.ds(pl.multiple_of(k * depth + i * fine, fine), fine)
                block = mbuf[slot, pl.ds(pl.multiple_of(i * fine, fine), fine)]
                acc[...] += jnp.dot(pat_v[:, cols], block, preferred_element_type=F32)
                wide = block.astype(F32).reshape(fine // 8, 8, width)
                sq[...] += jnp.sum(wide * wide, axis=0)
                return carry

            lax.fori_loop(0, depth // fine, inner, 0)

            @pl.when(j + slots < total_steps)
            def _():
                model_copy(j + slots).start()
            if early and c == chunks - 1:
                @pl.when(k >= steps - early)
                def _():
                    relay_slot(k - (steps - early))
            return carry

        lax.fori_loop(0, steps, body, 0)
        squares = jnp.sum(sq[...], axis=0, keepdims=True)
        for d in range(2):
            rows = pl.ds(d * half_rows, half_rows)
            phi = phi_ref[rows, 0:1]
            part[d, c] = beta * (phi * acc[rows] - (0.5 * phi * phi) * squares)

            @pl.when(hops[d] == 0)
            def _():
                for u in range(c * subs, (c + 1) * subs):
                    rs_copy(d, u).start()

    def later_slot(t, carry):
        relay_slot(t)
        return carry

    lax.fori_loop(early, units + 2 * (last - 1), later_slot, 0)

    def weight_block(g, u):
        c, s = u // subs, u % subs
        return (pl.ds(pl.multiple_of((1 - g) * half_rows + s * sub, sub), sub),
                pl.ds(pl.multiple_of(c * width, width), width))

    def agz_copy(g, u, sums=False):
        rows, cols = weight_block(g, u)
        ref = dpart.at[0, g] if sums else w_ref.at[0, rows, cols]
        return pltpu.make_async_remote_copy(
            src_ref=ref, dst_ref=ref, send_sem=agz_send.at[g, u], recv_sem=agz_recv.at[g, u],
            device_id={"pix": nexts[g]}, device_id_type=MESH)

    def ags_copy(g, u, sums=False):
        rows, cols = weight_block(g, u)
        src = dpart.at[0, g] if sums else w_ref.at[0, rows, cols]
        dst = dpart.at[1, g] if sums else w_ref.at[1, rows, cols]
        return pltpu.make_async_remote_copy(
            src_ref=src, dst_ref=dst, send_sem=ags_send.at[g, u], recv_sem=ags_recv.at[g, u],
            device_id={"pat": 1 - core}, device_id_type=MESH)

    def forward(g, u, sums=False):
        agz_copy(g, u, sums).wait_recv()

        @pl.when(hops[g] < last)
        def _():
            agz_copy(g, u, sums).start()
        ags_copy(g, u, sums).start()

    def st_copy(k):
        return pltpu.make_async_remote_copy(
            src_ref=st.at[0], dst_ref=st.at[k], send_sem=st_send.at[k], recv_sem=st_recv.at[k],
            device_id={"ori": lax.rem(ori + k, n_ori)}, device_id_type=MESH)

    for g in range(2):
        @pl.when(hops[g] == 0)
        def _():
            top = jnp.max(sc[...], axis=1, keepdims=True)
            total = jnp.sum(jnp.exp(sc[...] - top), axis=1, keepdims=True)
            lane = lax.broadcasted_iota(jnp.int32, (half_rows, 128), 1)
            packed = jnp.where(lane == 0, top, jnp.where(lane == 1, total, 0.0))
            st[0] = packed.T[0:8, :]
            for k in range(1, n_ori):
                st_copy(k).start()
            tops, totals = [top], [total]
            for k in range(1, n_ori):
                st_copy(k).wait_recv()
                other = jnp.concatenate(
                    [st[k], jnp.zeros((120, half_rows), F32)], axis=0).T
                tops.append(other[:, 0:1])
                totals.append(other[:, 1:2])
            most = functools.reduce(jnp.maximum, tops)
            whole = sum(t * jnp.exp(m - most) for m, t in zip(tops, totals))
            lse = most + jnp.log(whole)
            phi = phi_ref[(1 - g) * half_rows:(2 - g) * half_rows, 0:1]
            for c in range(chunks):
                cols = slice(c * width, (c + 1) * width)
                prob = jnp.exp(sc[:, cols] - lse)
                w_ref[0, (1 - g) * half_rows:(2 - g) * half_rows, cols] = (prob * phi).astype(BF16)
                dpart[0, g, :, cols] = jnp.sum(prob * (phi * phi), axis=0, keepdims=True)
                for u in range(c * subs, (c + 1) * subs):
                    agz_copy(g, u).start()
                    ags_copy(g, u).start()
            agz_copy(g, units, True).start()
            ags_copy(g, units, True).start()
            for k in range(1, n_ori):
                st_copy(k).wait_send()

    def gather_slot(t, carry):
        for g in range(2):
            u = t - 2 * (hops[g] - 1)

            @pl.when((hops[g] > 0) & (u >= 0) & (u < units))
            def _():
                forward(g, u)

            @pl.when((hops[g] > 0) & (u == units))
            def _():
                forward(g, units, True)
        return carry

    lax.fori_loop(0, units + 1 + 2 * (last - 1), gather_slot, 0)

    def each_unit(action):
        def step(u, carry):
            action(u)
            return carry
        lax.fori_loop(0, units, step, 0)

    for g in range(2):
        each_unit(lambda u: ags_copy(g, u).wait_recv())
        ags_copy(g, units, True).wait_recv()
    den_ref[...] = 1.0 / (prior_weight + (
        (dpart[0, 0] + dpart[0, 1]) + (dpart[1, 0] + dpart[1, 1])))

    for g in range(2):
        each_unit(lambda u: ags_copy(g, u).wait_send())
        ags_copy(g, units, True).wait_send()

        @pl.when(hops[g] < last)
        def _():
            each_unit(lambda u: rs_copy(g, u).wait_send())
            each_unit(lambda u: agz_copy(g, u).wait_send())
            agz_copy(g, units, True).wait_send()


def update_kernel(width, place_ref, pat_ref, first_ref, second_ref, inverse_ref, model_ref, out_ref):
    pats = pat_ref[...].T
    columns = out_ref.shape[1]
    for c in range(columns // width):
        cols = slice(c * width, (c + 1) * width)
        weights = jnp.concatenate([first_ref[0, :, cols], second_ref[0, :, cols]], axis=0)
        numer = jnp.dot(pats, weights, preferred_element_type=F32)
        numer += prior_weight * model_ref[:, cols].astype(F32)
        out_ref[:, cols] = (numer * inverse_ref[:, cols]).astype(BF16)


def local(n_pix, n_ori, patterns, model, scale_table, scale_index, weight_table, weight_class):
    rows, pixels = patterns.shape
    columns = model.shape[1]
    half_pix = pixels // 2
    phi = jnp.broadcast_to(table_lookup(scale_table, scale_index)[:, None], (rows, 128))
    logw = table_lookup(weight_table, weight_class)[None, :]
    beta = float(pixels * n_pix) ** (-0.5)
    width = block_of(columns, 512)
    chunks = columns // width
    depth = block_of(pixels, 2048)
    steps = pixels // depth
    slots = min(8, chunks * steps)
    half_rows = rows // 2
    subs = 8
    units = chunks * subs
    dma = pltpu.SemaphoreType.DMA
    any_spec = pl.BlockSpec(memory_space=pl.ANY)
    vmem_spec = pl.BlockSpec(memory_space=pltpu.VMEM)
    gathered = lax.all_gather(patterns, "pat", axis=0, tiled=True)
    weights, inverse = pl.pallas_call(
        functools.partial(score_kernel, n_pix, n_ori, beta, chunks, subs, width, steps, depth, slots),
        out_shape=(
            jax.ShapeDtypeStruct((2, rows, columns), BF16),
            jax.ShapeDtypeStruct((1, columns), F32),
        ),
        in_specs=[any_spec, any_spec, vmem_spec, vmem_spec],
        out_specs=(vmem_spec, vmem_spec),
        scratch_shapes=[
            pltpu.VMEM((rows, pixels), BF16),
            pltpu.VMEM((slots, depth, width), BF16),
            pltpu.VMEM((rows, width), F32),
            pltpu.VMEM((8, width), F32),
            pltpu.VMEM((2, chunks, half_rows, width), F32),
            pltpu.VMEM((2, chunks, half_rows, width), F32),
            pltpu.VMEM((half_rows, columns), F32),
            pltpu.VMEM((n_ori, 8, half_rows), F32),
            pltpu.VMEM((2, 2, 1, columns), F32),
            dma((steps,)),
            dma((slots,)),
            dma((2, units)),
            dma((2, units)),
            dma((n_ori,)),
            dma((n_ori,)),
            dma((2, units + 1)),
            dma((2, units + 1)),
            dma((2, units + 1)),
            dma((2, units + 1)),
        ],
        compiler_params=pltpu.CompilerParams(
            collective_id=0, has_side_effects=True, vmem_limit_bytes=56 * 2**20),
        cost_estimate=pl.CostEstimate(
            flops=2 * rows * pixels * columns,
            bytes_accessed=2 * pixels * (rows + columns), transcendentals=rows * columns),
    )(patterns, model, phi, logw)

    block = block_of(half_pix, 512)
    blocks = half_pix // block
    own_half = lax.axis_index("pat").astype(jnp.int32).reshape(1)
    return pl.pallas_call(
        functools.partial(update_kernel, block_of(columns, 256)),
        out_shape=jax.ShapeDtypeStruct((half_pix, columns), BF16),
        grid_spec=pltpu.PrefetchScalarGridSpec(
            num_scalar_prefetch=1,
            grid=(blocks,),
            in_specs=[
                pl.BlockSpec((2 * rows, block), lambda i, half: (0, half[0] * blocks + i)),
                pl.BlockSpec((1, rows, columns), lambda i, half: (half[0], 0, 0)),
                pl.BlockSpec((1, rows, columns), lambda i, half: (1 - half[0], 0, 0)),
                pl.BlockSpec((1, columns), lambda i, half: (0, 0)),
                pl.BlockSpec((block, columns), lambda i, half: (half[0] * blocks + i, 0)),
            ],
            out_specs=pl.BlockSpec((block, columns), lambda i, half: (i, 0)),
        ),
        compiler_params=pltpu.CompilerParams(vmem_limit_bytes=60 * 2**20),
        cost_estimate=pl.CostEstimate(
            flops=4 * rows * half_pix * columns,
            bytes_accessed=4 * half_pix * (rows + columns), transcendentals=0),
    )(own_half, gathered, weights, weights, inverse, model)


def solution(mesh):
    placed = (
        P(("grp", "pat"), "pix"),
        P(("grp", "pix"), "ori"),
        P("grp"),
        P(("grp", "pat")),
        P("grp"),
        P(("grp", "ori")),
    )
    return jax.shard_map(
        functools.partial(local, mesh.shape["pix"], mesh.shape["ori"]),
        mesh=mesh,
        in_specs=placed,
        out_specs=P(("grp", "pix", "pat"), "ori"),
        check_vma=False,
    )
```

```python
import functools

import jax
import jax.numpy as jnp
from jax import lax
from jax.experimental import pallas as pl
from jax.experimental.pallas import tpu as pltpu
from jax.sharding import PartitionSpec as P

prior_weight = 0.5
MESH = pl.DeviceIdType.MESH
F32 = jnp.float32
BF16 = jnp.bfloat16


def table_lookup(table, index):
    levels = jnp.arange(table.shape[0], dtype=jnp.int32)
    return jnp.sum(jnp.where(index[:, None] == levels[None, :], table[None, :], 0.0), axis=1)


def block_of(size, most):
    block = min(size, most)
    while size % block:
        block //= 2
    return block


def score_kernel(
    n_pix, n_ori, beta, chunks, subs, width, steps, depth, slots,
    pat_hbm, model_hbm, phi_ref, logw_ref,
    w_ref, den_ref,
    pat_v, mbuf, acc, sq, part, rx, sc, st, dpart,
    pat_sem, m_sem, rs_send, rs_recv, st_send, st_recv,
    agz_send, agz_recv, ags_send, ags_recv,
):
    z = lax.axis_index("pix")
    core = lax.axis_index("pat")
    ori = lax.axis_index("ori")
    last = n_pix - 1
    half_rows = part.shape[2]
    sub = half_rows // subs
    units = chunks * subs
    hops = (z, last - z)
    nexts = (lax.rem(z + 1, n_pix), lax.rem(z + n_pix - 1, n_pix))

    def model_copy(j):
        c, k = j // steps, j % steps
        return pltpu.make_async_copy(
            model_hbm.at[pl.ds(k * depth, depth), pl.ds(c * width, width)],
            mbuf.at[j % slots], m_sem.at[j % slots])

    def pattern_copy(k):
        cols = pl.ds(k * depth, depth)
        return pltpu.make_async_copy(pat_hbm.at[:, cols], pat_v.at[:, cols], pat_sem.at[k])

    total_steps = chunks * steps
    fine = block_of(depth, 2048)
    for k in range(steps):
        pattern_copy(k).start()
        if k < min(slots, total_steps):
            model_copy(k).start()
    for j in range(steps, min(slots, total_steps)):
        model_copy(j).start()

    barrier = pltpu.get_barrier_semaphore()
    for d in range(2):
        @pl.when(hops[d] < last)
        def _():
            pl.semaphore_signal(barrier, inc=1, device_id={"pix": nexts[d]}, device_id_type=MESH)
    pl.semaphore_signal(barrier, inc=1, device_id={"pat": 1 - core}, device_id_type=MESH)
    for k in range(1, n_ori):
        pl.semaphore_signal(
            barrier, inc=1, device_id={"ori": lax.rem(ori + k, n_ori)}, device_id_type=MESH)
    @pl.when(hops[0] * hops[1] == 0)
    def _():
        pl.semaphore_wait(barrier, n_ori + 1)

    @pl.when(hops[0] * hops[1] > 0)
    def _():
        pl.semaphore_wait(barrier, n_ori + 2)

    def rows_of(s):
        return pl.ds(pl.multiple_of(s * sub, sub), sub)

    def rs_copy(d, u):
        c, s = u // subs, u % subs
        return pltpu.make_async_remote_copy(
            src_ref=part.at[d, c, rows_of(s)], dst_ref=rx.at[d, c, rows_of(s)],
            send_sem=rs_send.at[d, u], recv_sem=rs_recv.at[d, u],
            device_id={"pix": nexts[d]}, device_id_type=MESH)

    def relay(d, u):
        c, s = u // subs, u % subs
        rs_copy(d, u).wait_recv()
        rows = rows_of(s)

        @pl.when(hops[d] < last)
        def _():
            part[d, c, rows] = part[d, c, rows] + rx[d, c, rows]
            rs_copy(d, u).start()

        @pl.when(hops[d] == last)
        def _():
            cols = pl.ds(pl.multiple_of(c * width, width), width)
            sc[rows, cols] = part[d, c, rows] + rx[d, c, rows] + logw_ref[:, cols]

    def relay_slot(t):
        for d in range(2):
            u = t - 2 * (hops[d] - 1)

            @pl.when((hops[d] > 0) & (u >= 0) & (u < units))
            def _():
                relay(d, u)

    early = (chunks - 1) * subs
    if early > steps:
        early = 0

    for c in range(chunks):
        acc[...] = jnp.zeros_like(acc)
        sq[...] = jnp.zeros_like(sq)

        def body(k, carry):
            j = c * steps + k
            slot = j % slots
            if c == 0:
                pattern_copy(k).wait()
            model_copy(j).wait()
            def inner(i, carry):
                cols = pl.ds(pl.multiple_of(k * depth + i * fine, fine), fine)
                block = mbuf[slot, pl.ds(pl.multiple_of(i * fine, fine), fine)]
                acc[...] += jnp.dot(pat_v[:, cols], block, preferred_element_type=F32)
                wide = block.astype(F32).reshape(fine // 8, 8, width)
                sq[...] += jnp.sum(wide * wide, axis=0)
                return carry

            lax.fori_loop(0, depth // fine, inner, 0)

            @pl.when(j + slots < total_steps)
            def _():
                model_copy(j + slots).start()
            if early and c == chunks - 1:
                @pl.when(k >= steps - early)
                def _():
                    relay_slot(k - (steps - early))
            return carry

        lax.fori_loop(0, steps, body, 0)
        squares = jnp.sum(sq[...], axis=0, keepdims=True)
        for d in range(2):
            rows = pl.ds(d * half_rows, half_rows)
            phi = phi_ref[rows, 0:1]
            part[d, c] = beta * (phi * acc[rows] - (0.5 * phi * phi) * squares)

            @pl.when(hops[d] == 0)
            def _():
                for u in range(c * subs, (c + 1) * subs):
                    rs_copy(d, u).start()

    def later_slot(t, carry):
        relay_slot(t)
        return carry

    lax.fori_loop(early, units + 2 * (last - 1), later_slot, 0)

    def weight_block(g, u):
        c, s = u // subs, u % subs
        return (pl.ds(pl.multiple_of((1 - g) * half_rows + s * sub, sub), sub),
                pl.ds(pl.multiple_of(c * width, width), width))

    def agz_copy(g, u, sums=False):
        rows, cols = weight_block(g, u)
        ref = dpart.at[0, g] if sums else w_ref.at[0, rows, cols]
        return pltpu.make_async_remote_copy(
            src_ref=ref, dst_ref=ref, send_sem=agz_send.at[g, u], recv_sem=agz_recv.at[g, u],
            device_id={"pix": nexts[g]}, device_id_type=MESH)

    def ags_copy(g, u, sums=False):
        rows, cols = weight_block(g, u)
        src = dpart.at[0, g] if sums else w_ref.at[0, rows, cols]
        dst = dpart.at[1, g] if sums else w_ref.at[1, rows, cols]
        return pltpu.make_async_remote_copy(
            src_ref=src, dst_ref=dst, send_sem=ags_send.at[g, u], recv_sem=ags_recv.at[g, u],
            device_id={"pat": 1 - core}, device_id_type=MESH)

    def forward(g, u, sums=False):
        agz_copy(g, u, sums).wait_recv()

        @pl.when(hops[g] < last)
        def _():
            agz_copy(g, u, sums).start()
        ags_copy(g, u, sums).start()

    def st_copy(k):
        return pltpu.make_async_remote_copy(
            src_ref=st.at[0], dst_ref=st.at[k], send_sem=st_send.at[k], recv_sem=st_recv.at[k],
            device_id={"ori": lax.rem(ori + k, n_ori)}, device_id_type=MESH)

    for g in range(2):
        @pl.when(hops[g] == 0)
        def _():
            top = jnp.max(sc[...], axis=1, keepdims=True)
            total = jnp.sum(jnp.exp(sc[...] - top), axis=1, keepdims=True)
            lane = lax.broadcasted_iota(jnp.int32, (half_rows, 128), 1)
            packed = jnp.where(lane == 0, top, jnp.where(lane == 1, total, 0.0))
            st[0] = packed.T[0:8, :]
            for k in range(1, n_ori):
                st_copy(k).start()
            tops, totals = [top], [total]
            for k in range(1, n_ori):
                st_copy(k).wait_recv()
                other = jnp.concatenate(
                    [st[k], jnp.zeros((120, half_rows), F32)], axis=0).T
                tops.append(other[:, 0:1])
                totals.append(other[:, 1:2])
            most = functools.reduce(jnp.maximum, tops)
            whole = sum(t * jnp.exp(m - most) for m, t in zip(tops, totals))
            lse = most + jnp.log(whole)
            phi = phi_ref[(1 - g) * half_rows:(2 - g) * half_rows, 0:1]
            for c in range(chunks):
                cols = slice(c * width, (c + 1) * width)
                prob = jnp.exp(sc[:, cols] - lse)
                w_ref[0, (1 - g) * half_rows:(2 - g) * half_rows, cols] = (prob * phi).astype(BF16)
                dpart[0, g, :, cols] = jnp.sum(prob * (phi * phi), axis=0, keepdims=True)
                for u in range(c * subs, (c + 1) * subs):
                    agz_copy(g, u).start()
                    ags_copy(g, u).start()
            agz_copy(g, units, True).start()
            ags_copy(g, units, True).start()
            for k in range(1, n_ori):
                st_copy(k).wait_send()

    lag = 4

    def gather_slot(t, carry):
        for g in range(2):
            u = t - lag * (hops[g] - 1)

            @pl.when((hops[g] > 0) & (u >= 0) & (u < units))
            def _():
                forward(g, u)

            @pl.when((hops[g] > 0) & (u == units))
            def _():
                forward(g, units, True)
        return carry

    lax.fori_loop(0, units + 1 + lag * (last - 1), gather_slot, 0)

    def each_unit(action):
        def step(u, carry):
            action(u)
            return carry
        lax.fori_loop(0, units, step, 0)

    for g in range(2):
        each_unit(lambda u: ags_copy(g, u).wait_recv())
        ags_copy(g, units, True).wait_recv()
    den_ref[...] = 1.0 / (prior_weight + (
        (dpart[0, 0] + dpart[0, 1]) + (dpart[1, 0] + dpart[1, 1])))

    for g in range(2):
        each_unit(lambda u: ags_copy(g, u).wait_send())
        ags_copy(g, units, True).wait_send()

        @pl.when(hops[g] < last)
        def _():
            each_unit(lambda u: rs_copy(g, u).wait_send())
            each_unit(lambda u: agz_copy(g, u).wait_send())
            agz_copy(g, units, True).wait_send()


def update_kernel(width, tall, place_ref, pat_ref, first_ref, second_ref, inverse_ref, model_ref, out_ref):
    pixels, columns = out_ref.shape
    count = columns // width
    deep = pat_ref.shape[0] // count

    def turned(p, c):
        return pat_ref[c * deep:(c + 1) * deep, p * tall:(p + 1) * tall].T

    pieces = [turned(0, c) for c in range(count)]
    for p in range(pixels // tall):
        pats = jnp.concatenate(pieces, axis=1)
        pieces = []
        here = slice(p * tall, (p + 1) * tall)
        for c in range(count):
            cols = slice(c * width, (c + 1) * width)
            weights = jnp.concatenate([first_ref[0, :, cols], second_ref[0, :, cols]], axis=0)
            numer = jnp.dot(pats, weights, preferred_element_type=F32)
            if (p + 1) * tall < pixels:
                pieces.append(turned(p + 1, c))
            numer += prior_weight * model_ref[here, cols].astype(F32)
            out_ref[here, cols] = (numer * inverse_ref[:, cols]).astype(BF16)


def local(n_pix, n_ori, patterns, model, scale_table, scale_index, weight_table, weight_class):
    rows, pixels = patterns.shape
    columns = model.shape[1]
    half_pix = pixels // 2
    phi = jnp.broadcast_to(table_lookup(scale_table, scale_index)[:, None], (rows, 128))
    logw = table_lookup(weight_table, weight_class)[None, :]
    beta = float(pixels * n_pix) ** (-0.5)
    width = block_of(columns, 512)
    chunks = columns // width
    depth = block_of(pixels, 2048)
    steps = pixels // depth
    slots = min(8, chunks * steps)
    half_rows = rows // 2
    subs = 8
    units = chunks * subs
    dma = pltpu.SemaphoreType.DMA
    any_spec = pl.BlockSpec(memory_space=pl.ANY)
    vmem_spec = pl.BlockSpec(memory_space=pltpu.VMEM)
    gathered = lax.all_gather(patterns, "pat", axis=0, tiled=True)
    weights, inverse = pl.pallas_call(
        functools.partial(score_kernel, n_pix, n_ori, beta, chunks, subs, width, steps, depth, slots),
        out_shape=(
            jax.ShapeDtypeStruct((2, rows, columns), BF16),
            jax.ShapeDtypeStruct((1, columns), F32),
        ),
        in_specs=[any_spec, any_spec, vmem_spec, vmem_spec],
        out_specs=(vmem_spec, vmem_spec),
        scratch_shapes=[
            pltpu.VMEM((rows, pixels), BF16),
            pltpu.VMEM((slots, depth, width), BF16),
            pltpu.VMEM((rows, width), F32),
            pltpu.VMEM((8, width), F32),
            pltpu.VMEM((2, chunks, half_rows, width), F32),
            pltpu.VMEM((2, chunks, half_rows, width), F32),
            pltpu.VMEM((half_rows, columns), F32),
            pltpu.VMEM((n_ori, 8, half_rows), F32),
            pltpu.VMEM((2, 2, 1, columns), F32),
            dma((steps,)),
            dma((slots,)),
            dma((2, units)),
            dma((2, units)),
            dma((n_ori,)),
            dma((n_ori,)),
            dma((2, units + 1)),
            dma((2, units + 1)),
            dma((2, units + 1)),
            dma((2, units + 1)),
        ],
        compiler_params=pltpu.CompilerParams(
            collective_id=0, has_side_effects=True, vmem_limit_bytes=56 * 2**20),
        cost_estimate=pl.CostEstimate(
            flops=2 * rows * pixels * columns,
            bytes_accessed=2 * pixels * (rows + columns), transcendentals=rows * columns),
    )(patterns, model, phi, logw)

    block = block_of(half_pix, 1024)
    blocks = half_pix // block
    own_half = lax.axis_index("pat").astype(jnp.int32).reshape(1)
    return pl.pallas_call(
        functools.partial(update_kernel, block_of(columns, 256), block_of(block, 512)),
        out_shape=jax.ShapeDtypeStruct((half_pix, columns), BF16),
        grid_spec=pltpu.PrefetchScalarGridSpec(
            num_scalar_prefetch=1,
            grid=(blocks,),
            in_specs=[
                pl.BlockSpec((2 * rows, block), lambda i, half: (0, half[0] * blocks + i)),
                pl.BlockSpec((1, rows, columns), lambda i, half: (half[0], 0, 0)),
                pl.BlockSpec((1, rows, columns), lambda i, half: (1 - half[0], 0, 0)),
                pl.BlockSpec((1, columns), lambda i, half: (0, 0)),
                pl.BlockSpec((block, columns), lambda i, half: (half[0] * blocks + i, 0)),
            ],
            out_specs=pl.BlockSpec((block, columns), lambda i, half: (i, 0)),
        ),
        compiler_params=pltpu.CompilerParams(vmem_limit_bytes=60 * 2**20),
        cost_estimate=pl.CostEstimate(
            flops=4 * rows * half_pix * columns,
            bytes_accessed=4 * half_pix * (rows + columns), transcendentals=0),
    )(own_half, gathered, weights, weights, inverse, model)


def solution(mesh):
    placed = (
        P(("grp", "pat"), "pix"),
        P(("grp", "pix"), "ori"),
        P("grp"),
        P(("grp", "pat")),
        P("grp"),
        P(("grp", "ori")),
    )
    return jax.shard_map(
        functools.partial(local, mesh.shape["pix"], mesh.shape["ori"]),
        mesh=mesh,
        in_specs=placed,
        out_specs=P(("grp", "pix", "pat"), "ori"),
        check_vma=False,
    )
```
